128 devices in a mesh: row: 8 (over z, core), col: 16 (over y, x).
Axes of the slice: x: 4, y: 4, z: 4, core: 2. Of those that a mesh axis runs over, the one named last changes fastest.
Arguments:
- counts: int32 [16384, 32768], P('row', 'col'), may hold values from 0 to 512
- block_mask: int32 [64, 128], P('row', 'col'), may hold values from 0 to 1
- row_perm: int32 [16384], P('row'), may hold values from 0 to 16383, as said below
- col_perm: int32 [32768], P('col'), may hold values from 0 to 32767, as said below
- row_logm: float32 [16384], P('row'), may hold values from 0 to 3
- col_logm: float32 [32768], P('col'), may hold values from 0 to 3
- row_emb: bfloat16 [16384, 512], P(('row', 'col')), may hold values from -1.1953125 to 1.1953125
- col_emb: bfloat16 [32768, 512], P(('col', 'row')), may hold values from -1.1953125 to 1.1953125
Outputs:
- row_grad: float32 [16384, 512], P(('row', 'col'))
- col_grad: float32 [32768, 512], P(('col', 'row'))
The draws below stay inside these ranges and needn't reach their ends.
Inputs may be any that keep to these rules, and one draw needn't show every extreme that they name: `row_perm`: each aligned block of 2048 entries is a permutation of that block's own index range. `col_perm`: each aligned block of 2048 entries is a permutation of that block's own index range.
All inputs are finite; a program needn't handle non-finite values.
Results may differ from the reference program's by a relative error of at most 0.0022.
Values may be sent and summed in bfloat16 or wider, within the bound.
A program may use at most 128 MiB of HBM per device.

```python
import jax
import jax.numpy as jnp
from jax import lax

D = 512
SR = 2048
SC = 2048
BLK = 256
ROWS = 16384
COLS = 32768
N_ROW = 8


def draw_counts(key, part):
    key = jax.random.fold_in(key, 11)
    first, second, third = jax.random.split(key, 3)
    present = jax.random.randint(first, (ROWS, COLS), 0, 2)
    expo = jax.random.randint(second, (ROWS, COLS), 0, 10)
    upper = jnp.left_shift(jnp.ones((ROWS, COLS), jnp.int32), expo) + 1
    value = jax.random.randint(third, (ROWS, COLS), 1, upper)
    return (present * value).astype(jnp.int32)


def draw_block_mask(key, part):
    key = jax.random.fold_in(key, 12)
    first, second = jax.random.split(key)
    groups_r = ROWS // SR
    groups_c = COLS // SC
    level = jax.random.randint(first, (groups_r, 1, groups_c, 1), 1, 5)
    pick = jax.random.randint(second, (groups_r, SR // BLK, groups_c, SC // BLK), 0, 4)
    return (pick < level).astype(jnp.int32).reshape(ROWS // BLK, COLS // BLK)


def block_perms(key, total, block):
    groups = total // block
    keys = jax.random.split(key, groups)
    perms = jax.vmap(lambda single: jax.random.permutation(single, block))(keys)
    perms = perms + (jnp.arange(groups, dtype=jnp.int32) * block)[:, None]
    return perms.reshape(total).astype(jnp.int32)


def draw_row_perm(key, part):
    key = jax.random.fold_in(key, 13)
    return block_perms(key, ROWS, SR)


def draw_col_perm(key, part):
    key = jax.random.fold_in(key, 14)
    return block_perms(key, COLS, SC)


def steps_of(key, extent, cuts, smallest, high):
    def one(axis_at, parts):
        draws = jax.random.uniform(jax.random.fold_in(jax.random.fold_in(key, 6), axis_at), (parts,), jnp.float32, smallest / len(cuts), high / len(cuts))
        return jnp.repeat(jnp.exp(draws), extent[axis_at] // parts).reshape((-1,) + (1,) * (len(extent) - axis_at - 1))

    factor_of = one(*cuts[0])
    for cut in cuts[1:]:
        factor_of = factor_of * one(*cut)
    return factor_of


def noise(key, shape, spread, reach, cuts=(), kind=jnp.bfloat16):
    values = spread * jax.random.normal(key, shape, jnp.float32)
    if cuts:
        values = values * steps_of(key, shape, cuts, -0.22, 0.18)
    return jnp.clip(values, -reach, reach).astype(kind)


def setup_inputs(seed: int = 0) -> dict:
    seeds = jax.random.split(jax.random.key(seed), 9)
    return {
        "counts": draw_counts(jax.random.fold_in(seeds[8], 71), 0),
        "block_mask": draw_block_mask(jax.random.fold_in(seeds[8], 71), 0),
        "row_perm": draw_row_perm(jax.random.fold_in(seeds[8], 71), 0),
        "col_perm": draw_col_perm(jax.random.fold_in(seeds[8], 71), 0),
        "row_logm": jnp.clip(3.0 * jax.random.uniform(seeds[4], (ROWS,), jnp.float32) ** steps_of(seeds[4], (ROWS,), ((0, 8),), -0.2, 0.2), 0.0, 3.0),
        "col_logm": jnp.clip(3.0 * jax.random.uniform(seeds[5], (COLS,), jnp.float32) ** steps_of(seeds[5], (COLS,), ((0, 16),), -0.2, 0.2), 0.0, 3.0),
        "row_emb": noise(seeds[6], (ROWS, D), 0.2, 1.1953125, ((0, 128),)),
        "col_emb": noise(seeds[7], (COLS, D), 0.2, 1.1953125, ((0, 128),)),
    }


def cell_delta(score, count, active, row_part, col_part):
    real_count = count.astype(jnp.float32)
    safe = jnp.maximum(real_count, 1.0)
    pmi = jnp.log(safe) - row_part[:, None] - col_part[None, :]
    confid = 0.1 + 0.25 * jnp.sqrt(safe)
    positive = confid * (score - pmi)
    zeroed = jax.nn.sigmoid(score - pmi)
    deriv = jnp.where(count > 0, positive, zeroed)
    return (active.astype(jnp.float32) * deriv).astype(jnp.bfloat16)

def reference(counts, block_mask, row_perm, col_perm, row_logm, col_logm, row_emb, col_emb):
    cvec = col_emb[col_perm]
    col_active = jnp.repeat(block_mask, BLK, axis=1)

    def group_step(accum, inputs):
        count_rows, mask_rows, perm_rows, logm_rows = inputs
        wvec = row_emb[perm_rows]
        score = lax.dot_general(wvec, cvec, (((1,), (1,)), ((), ())), preferred_element_type=jnp.float32)
        active = jnp.repeat(mask_rows, BLK, axis=0)
        delta = cell_delta(score, count_rows, active, logm_rows, col_logm)
        gshard = jnp.dot(delta, cvec, preferred_element_type=jnp.float32) / jnp.sqrt(jnp.float32(COLS))
        hpart = lax.dot_general(delta, wvec, (((0,), (0,)), ((), ())), preferred_element_type=jnp.float32)
        return (accum + hpart, gshard)
    inputs = (counts.reshape(N_ROW, SR, COLS), col_active.reshape(N_ROW, SR // BLK, COLS), row_perm.reshape(N_ROW, SR), row_logm.reshape(N_ROW, SR))
    start = jnp.zeros((COLS, D), jnp.float32)
    hsum, gparts = lax.scan(group_step, start, inputs)
    gshard = gparts.reshape(ROWS, D)
    hshard = hsum / jnp.sqrt(jnp.float32(ROWS))
    row_grad = jnp.zeros((ROWS, D), jnp.float32).at[row_perm].set(gshard)
    col_grad = jnp.zeros((COLS, D), jnp.float32).at[col_perm].set(hshard)
    return (row_grad, col_grad)
```

```python
import functools

import jax
import jax.numpy as jnp
from jax import lax
from jax.experimental import pallas as pl
from jax.experimental.pallas import tpu as pltpu
from jax.sharding import PartitionSpec as P

MESH = pl.DeviceIdType.MESH
F32 = jnp.float32
BF16 = jnp.bfloat16

SR = 2048
D = 512
HALF = 256
BLK = 256
T = 512
NT = (((1,), (1,)), ((), ()))
NN = (((1,), (0,)), ((), ()))


def dot(a, b, dims):
    return lax.dot_general(a, b, dims, preferred_element_type=F32)


def kernel(
    g_scale, h_scale,
    counts, mask, rperm, cperm, rlog, clog, remb, cemb,
    rout, cout,
    cbuf, rg, cg, vec, vcol, wvec, wt, cvec, delta,
    gs, gord, r1, s2, r2,
    hown, hsend, hrecv, hb, hord, rz, fsend, frecv,
    csem, xs, xr, ys, yr, zs, zr, ks, kr, lsem,
    g1s, g1r, g2s, g2r, hks, hkr, hzs, hzr, fsm, frm,
):
    row = lax.axis_index("row")
    col = lax.axis_index("col")
    z, core = row // 2, row % 2
    y, x = col // 4, col % 4
    row0, col0 = row * SR, col * SR

    def dev(zz, kk, yy, xx):
        return ((zz % 4) * 2 + kk, (yy % 4) * 4 + (xx % 4))

    def at_x(d):
        return dev(z, core, y, x + d)

    def at_y(d):
        return dev(z, core, y + d, x)

    def at_z(d):
        return dev(z + d, core, y, x)

    sibling = dev(z, 1 - core, y, x)

    def send(src, dst, ssem, rsem, to):
        c = pltpu.make_async_remote_copy(
            src_ref=src, dst_ref=dst, send_sem=ssem, recv_sem=rsem, device_id=to, device_id_type=MESH
        )
        c.start()
        return c

    def got(ref, rsem, ssem):
        pltpu.make_async_remote_copy(
            src_ref=ref, dst_ref=ref, send_sem=ssem, recv_sem=rsem, device_id=sibling, device_id_type=MESH
        ).wait_recv()

    loads = []
    for i in range(4):
        c = pltpu.make_async_copy(counts.at[pl.ds(i * T, T)], cbuf.at[pl.ds(i * T, T)], csem.at[i])
        c.start()
        loads.append(c)

    barrier = pltpu.get_barrier_semaphore()
    partners = [at_x(d) for d in (1, 2, 3)] + [at_y(d) for d in (1, 2, 3)] + [at_z(d) for d in (1, 2, 3)] + [sibling]
    for to in partners:
        pl.semaphore_signal(barrier, inc=1, device_id=to, device_id_type=MESH)
    pl.semaphore_wait(barrier, len(partners))

    sent = []

    def zblk(d):
        return cg.at[(z + d) % 4, core]

    own_c = pltpu.make_async_copy(cemb, zblk(0), lsem.at[0])
    own_c.start()
    own_rows = []
    for h in range(2):
        c = pltpu.make_async_copy(remb.at[pl.ds(64 * h, 64)], rg.at[y, x, h], lsem.at[1 + h])
        c.start()
        own_rows.append(c)
    sent.append(send(cemb, zblk(0), zs.at[0], zr.at[0], at_z(1)))
    sent.append(send(cemb, zblk(0), zs.at[1], zr.at[1], at_z(3)))
    sent.append(send(cemb, zblk(0), ks.at[0], kr.at[0], sibling))

    def blk(h, first, second):
        if h == 0:
            return rg.at[(y + second) % 4, (x + first) % 4, h]
        return rg.at[(y + first) % 4, (x + second) % 4, h]

    def first_axis(h, d):
        return at_x(d) if h == 0 else at_y(d)

    def second_axis(h, d):
        return at_y(d) if h == 0 else at_x(d)

    for h in range(2):
        own = remb.at[pl.ds(64 * h, 64)]
        sent.append(send(own, blk(h, 0, 0), xs.at[h, 0], xr.at[h, 0], first_axis(h, 1)))
        sent.append(send(own, blk(h, 0, 0), xs.at[h, 1], xr.at[h, 1], first_axis(h, 3)))
    for h in range(2):
        own = remb.at[pl.ds(64 * h, 64)]
        sent.append(send(own, blk(h, 0, 0), ys.at[h, 0, 0], yr.at[h, 0, 0], second_axis(h, 1)))
        sent.append(send(own, blk(h, 0, 0), ys.at[h, 0, 1], yr.at[h, 0, 1], second_axis(h, 3)))

    lo, hi = pl.ds(0, 32), pl.ds(32, 32)
    for h in range(2):
        got(blk(h, 3, 0), xr.at[h, 0], xs.at[h, 0])
        sent.append(send(blk(h, 3, 0).at[lo], blk(h, 3, 0).at[lo], xs.at[h, 2], xr.at[h, 2], first_axis(h, 1)))
        got(blk(h, 1, 0), xr.at[h, 1], xs.at[h, 1])
        sent.append(send(blk(h, 1, 0).at[hi], blk(h, 1, 0).at[hi], xs.at[h, 3], xr.at[h, 3], first_axis(h, 3)))
    for h in range(2):
        for k, f in ((1, 3), (2, 1)):
            sent.append(send(blk(h, f, 0), blk(h, f, 0), ys.at[h, k, 0], yr.at[h, k, 0], second_axis(h, 1)))
            sent.append(send(blk(h, f, 0), blk(h, f, 0), ys.at[h, k, 1], yr.at[h, k, 1], second_axis(h, 3)))
    zlo, zhi = pl.ds(0, 128), pl.ds(128, 128)
    got(zblk(3), zr.at[0], zs.at[0])
    sent.append(send(zblk(3).at[zlo], zblk(3).at[zlo], zs.at[2], zr.at[2], at_z(1)))
    sent.append(send(zblk(3), zblk(3), ks.at[1], kr.at[1], sibling))
    got(zblk(1), zr.at[1], zs.at[1])
    sent.append(send(zblk(1).at[zhi], zblk(1).at[zhi], zs.at[3], zr.at[3], at_z(3)))
    sent.append(send(zblk(1), zblk(1), ks.at[2], kr.at[2], sibling))
    for h in range(2):
        got(blk(h, 2, 0).at[lo], xr.at[h, 2], xs.at[h, 2])
        got(blk(h, 2, 0).at[hi], xr.at[h, 3], xs.at[h, 3])
        sent.append(send(blk(h, 2, 0), blk(h, 2, 0), ys.at[h, 3, 0], yr.at[h, 3, 0], second_axis(h, 1)))
        sent.append(send(blk(h, 2, 0), blk(h, 2, 0), ys.at[h, 3, 1], yr.at[h, 3, 1], second_axis(h, 3)))
    firsts = (0, 3, 1, 2)
    for k in range(4):
        for h in range(2):
            f = firsts[k]
            got(blk(h, f, 3), yr.at[h, k, 0], ys.at[h, k, 0])
            sent.append(send(blk(h, f, 3).at[lo], blk(h, f, 3).at[lo], ys.at[h, k, 2], yr.at[h, k, 2], second_axis(h, 1)))
            got(blk(h, f, 1), yr.at[h, k, 1], ys.at[h, k, 1])
            sent.append(send(blk(h, f, 1).at[hi], blk(h, f, 1).at[hi], ys.at[h, k, 3], yr.at[h, k, 3], second_axis(h, 3)))
    got(zblk(2).at[zlo], zr.at[2], zs.at[2])
    got(zblk(2).at[zhi], zr.at[3], zs.at[3])
    sent.append(send(zblk(2), zblk(2), ks.at[3], kr.at[3], sibling))

    vec[...] = jnp.zeros_like(vec)
    vec[0:1, :] = (rperm[...] - row0).astype(F32)
    vec[1:2, :] = (cperm[...] - col0).astype(F32)
    vec[2:3, :] = rlog[...]

    def turn(i, _):
        o = pl.multiple_of(i * 128, 128)
        vcol[pl.ds(o, 128), :] = jnp.transpose(vec[:, pl.ds(o, 128)])
        return 0

    lax.fori_loop(0, 16, turn, 0)

    own_c.wait()
    for k, d in enumerate((0, 3, 1, 2)):
        got(cg.at[(z + d) % 4, 1 - core], kr.at[k], ks.at[k])

    lane = lax.broadcasted_iota(jnp.int32, (T, SR), 1).astype(F32)

    def pick(i, which, src):
        o = pl.multiple_of(i * T, T)
        hot = jnp.where(vcol[pl.ds(o, T), which : which + 1] == lane, 1.0, 0.0).astype(BF16)
        return dot(hot, src, NN).astype(BF16)

    def pick_c(i, _):
        cvec[pl.ds(pl.multiple_of(i * T, T), T), :] = pick(i, 1, cg[...].reshape(SR, D))
        return 0

    lax.fori_loop(0, 4, pick_c, 0)

    for c in own_rows:
        c.wait()
    for k in range(4):
        for h in range(2):
            f = firsts[k]
            got(blk(h, f, 2).at[lo], yr.at[h, k, 2], ys.at[h, k, 2])
            got(blk(h, f, 2).at[hi], yr.at[h, k, 3], ys.at[h, k, 3])

    def pick_w(i, _):
        o = pl.multiple_of(i * T, T)
        w = pick(i, 0, rg[...].reshape(SR, D))
        wvec[pl.ds(o, T), :] = w
        for h in range(2):
            wt[(core + h) % 2, :, pl.ds(o, T)] = jnp.transpose(w[:, HALF * h : HALF * (h + 1)])
        return 0

    lax.fori_loop(0, 4, pick_w, 0)

    for c in loads:
        c.wait()

    def cells(t, _):
        i, j = t // 4, t % 4
        ro = pl.multiple_of(i * T, T)
        co = pl.multiple_of(j * T, T)
        score = dot(wvec[pl.ds(ro, T), :], cvec[pl.ds(co, T), :], NT)
        for a in range(2):
            for b in range(2):
                ra = pl.multiple_of(ro + a * BLK, BLK)
                cb = pl.multiple_of(co + b * BLK, BLK)
                count = cbuf[pl.ds(ra, BLK), pl.ds(cb, BLK)].astype(F32)
                safe = jnp.maximum(count, 1.0)
                base = vcol[pl.ds(ra, BLK), 2:3] + clog[:, pl.ds(cb, BLK)]
                u = score[a * BLK : (a + 1) * BLK, b * BLK : (b + 1) * BLK] - (jnp.log(safe) - base)
                pos = (0.1 + 0.25 * (safe * lax.rsqrt(safe))) * u
                zero = 0.5 * jnp.tanh(0.5 * u) + 0.5
                on = mask[i * 2 + a, j * 2 + b].astype(F32)
                delta[pl.ds(ra, BLK), pl.ds(cb, BLK)] = (on * jnp.where(count > 0.0, pos, zero)).astype(BF16)
        return 0

    lax.fori_loop(0, 16, cells, 0)

    kcopies = []
    for j in range(4):
        js = pl.ds(j * T, T)
        ht = dot(wt[...].reshape(D, SR), delta[:, js], NN) * h_scale
        hown[j] = ht[:HALF]
        hsend[j] = ht[HALF:]
        kcopies.append(send(hsend.at[j], hrecv.at[j], hks.at[j], hkr.at[j], sibling))
    sent += kcopies

    sub = lax.broadcasted_iota(jnp.int32, (T, SR), 0).astype(F32)

    def spread(k, which):
        at = vec[which : which + 1, :] - lax.convert_element_type(k * T, F32)
        return jnp.where(sub == at, 1.0, 0.0).astype(BF16)

    def row_terms(ch):
        def terms(i, _):
            o = pl.multiple_of(i * T, T)
            gs[pl.ds(o, T), :] = (
                dot(delta[pl.ds(o, T), :], cvec[:, HALF * ch : HALF * (ch + 1)], NN) * g_scale
            ).astype(BF16)
            return 0

        lax.fori_loop(0, 4, terms, 0)

        def order(k, _):
            gord[ch, k] = dot(spread(k, 0), gs[...], NN).astype(BF16).reshape(4, 2, 64, HALF)
            return 0

        lax.fori_loop(0, 4, order, 0)
        for d in (2, 1, 3):
            sent.append(send(gord.at[ch, (y + d) % 4, :, 0], r1.at[ch, 0, d - 1], g1s.at[ch, 0, d - 1], g1r.at[ch, 0, d - 1], at_y(d)))
            sent.append(send(gord.at[ch, :, (x + d) % 4, 1], r1.at[ch, 1, d - 1], g1s.at[ch, 1, d - 1], g1r.at[ch, 1, d - 1], at_x(d)))

    row_terms(0)

    for j in range(4):
        got(hrecv.at[j], hkr.at[j], hks.at[j])
        hb[:, j * T : (j + 1) * T] = (hown[j] + hrecv[j]).astype(BF16)

    def order_c(k, _):
        hord[k] = dot(spread(k, 1), hb[...], NT).astype(BF16).reshape(2, BLK, HALF)
        return 0

    lax.fori_loop(0, 4, order_c, 0)
    for d in (2, 1, 3):
        sent.append(send(hord.at[(z + d) % 4], rz.at[d - 1], hzs.at[d - 1], hzr.at[d - 1], at_z(d)))

    row_terms(1)

    def row_sums(ch):
        for h in range(2):
            for d in range(3):
                got(r1.at[ch, h, d], g1r.at[ch, h, d], g1s.at[ch, h, d])
            mine = gord[ch, y, :, 0] if h == 0 else gord[ch, :, x, 1]
            total = mine.astype(F32)
            for d in range(3):
                total = total + r1[ch, h, d].astype(F32)
            s2[ch, h] = total
            here = x if h == 0 else y
            for d in (2, 1, 3):
                sent.append(send(s2.at[ch, h, (here + d) % 4], r2.at[ch, h, d - 1], g2s.at[ch, h, d - 1], g2r.at[ch, h, d - 1], second(h, d)))

    def second(h, d):
        return at_x(d) if h == 0 else at_y(d)

    row_sums(0)
    row_sums(1)

    for d in range(3):
        got(rz.at[d], hzr.at[d], hzs.at[d])

    def col_total(k):
        total = hord[z, k].astype(F32)
        for d in range(3):
            total = total + rz[d, k].astype(F32)
        return total

    fsend[...] = col_total(1 - core)
    sent.append(send(fsend, frecv, fsm, frm, sibling))
    cout[core] = col_total(core)

    for ch in range(2):
        for h in range(2):
            for d in range(3):
                got(r2.at[ch, h, d], g2r.at[ch, h, d], g2s.at[ch, h, d])
            here = x if h == 0 else y
            total = s2[ch, h, here]
            for d in range(3):
                total = total + r2[ch, h, d]
            rout[h * 64 : (h + 1) * 64, ch * HALF : (ch + 1) * HALF] = total

    got(frecv, frm, fsm)
    cout[1 - core] = frecv[...]
    for c in sent:
        c.wait_send()


def shards(counts, block_mask, row_perm, col_perm, row_logm, col_logm, row_emb, col_emb):
    all_cols = counts.shape[1] * lax.axis_size("col")
    all_rows = counts.shape[0] * lax.axis_size("row")
    vm = pl.BlockSpec(memory_space=pltpu.VMEM)
    dma = pltpu.SemaphoreType.DMA
    V = pltpu.VMEM
    rout, cout = pl.pallas_call(
        functools.partial(kernel, float(all_cols) ** -0.5, float(all_rows) ** -0.5),
        out_shape=(
            jax.ShapeDtypeStruct((128, D), F32),
            jax.ShapeDtypeStruct((2, BLK, HALF), F32),
        ),
        in_specs=[pl.BlockSpec(memory_space=pl.ANY), pl.BlockSpec(memory_space=pltpu.SMEM)] + [vm] * 6,
        out_specs=(vm, vm),
        scratch_shapes=[
            V((SR, SR), jnp.int32),
            V((4, 4, 2, 64, D), BF16),
            V((4, 2, BLK, D), BF16),
            V((8, SR), F32),
            V((SR, 8), F32),
            V((SR, D), BF16),
            V((2, HALF, SR), BF16),
            V((SR, D), BF16),
            V((SR, SR), BF16),
            V((SR, HALF), BF16),
            V((2, 4, 4, 2, 64, HALF), BF16),
            V((2, 2, 3, 4, 64, HALF), BF16),
            V((2, 2, 4, 64, HALF), F32),
            V((2, 2, 3, 64, HALF), F32),
            V((4, HALF, T), F32),
            V((4, HALF, T), F32),
            V((4, HALF, T), F32),
            V((HALF, SR), BF16),
            V((4, 2, BLK, HALF), BF16),
            V((3, 2, BLK, HALF), BF16),
            V((BLK, HALF), F32),
            V((BLK, HALF), F32),
            dma((4,)),
            dma((2, 4)), dma((2, 4)),
            dma((2, 4, 4)), dma((2, 4, 4)),
            dma((4,)), dma((4,)),
            dma((4,)), dma((4,)),
            dma((3,)),
            dma((2, 2, 3)), dma((2, 2, 3)),
            dma((2, 2, 3)), dma((2, 2, 3)),
            dma((4,)), dma((4,)),
            dma((3,)), dma((3,)),
            dma, dma,
        ],
        compiler_params=pltpu.CompilerParams(
            collective_id=0, has_side_effects=True, vmem_limit_bytes=63 * 1024 * 1024
        ),
        cost_estimate=pl.CostEstimate(flops=26_000_000_000, bytes_accessed=20_000_000, transcendentals=12_000_000),
    )(
        counts, block_mask, row_perm.reshape(1, SR), col_perm.reshape(1, SR),
        row_logm.reshape(1, SR), col_logm.reshape(1, SR), row_emb, col_emb,
    )
    return rout, cout.transpose(1, 0, 2).reshape(BLK, D)


def solution(mesh):
    in_specs = (
        P("row", "col"),
        P("row", "col"),
        P("row"),
        P("col"),
        P("row"),
        P("col"),
        P(("row", "col"), None),
        P(("col", "row"), None),
    )
    out_specs = (P(("row", "col"), None), P(("col", "row"), None))
    return jax.shard_map(shards, mesh=mesh, in_specs=in_specs, out_specs=out_specs, check_vma=False)
```

```python
import functools

import jax
import jax.numpy as jnp
from jax import lax
from jax.experimental import pallas as pl
from jax.experimental.pallas import tpu as pltpu
from jax.sharding import PartitionSpec as P

MESH = pl.DeviceIdType.MESH
F32 = jnp.float32
BF16 = jnp.bfloat16

SR = 2048
D = 512
HALF = 256
BLK = 256
T = 512
NT = (((1,), (1,)), ((), ()))
NN = (((1,), (0,)), ((), ()))


def dot(a, b, dims):
    return lax.dot_general(a, b, dims, preferred_element_type=F32)


def kernel(
    g_scale, h_scale,
    counts, mask, rperm, cperm, rlog, clog, remb, cemb,
    rout, cout,
    cbuf, rg, cg, vec, vcol, wvec, wt, cvec, delta,
    gs, gord, r1, s2, s2b, r2,
    hown, hsend, hrecv, hb, hord, rz, fsend, frecv,
    csem, xs, xr, ys, yr, zs, zr, ks, kr, lsem,
    g1s, g1r, g2s, g2r, hks, hkr, hzs, hzr, fsm, frm,
):
    row = lax.axis_index("row")
    col = lax.axis_index("col")
    z, core = row // 2, row % 2
    y, x = col // 4, col % 4
    row0, col0 = row * SR, col * SR

    def dev(zz, kk, yy, xx):
        return ((zz % 4) * 2 + kk, (yy % 4) * 4 + (xx % 4))

    def at_x(d):
        return dev(z, core, y, x + d)

    def at_y(d):
        return dev(z, core, y + d, x)

    def at_z(d):
        return dev(z + d, core, y, x)

    sibling = dev(z, 1 - core, y, x)

    def send(src, dst, ssem, rsem, to):
        c = pltpu.make_async_remote_copy(
            src_ref=src, dst_ref=dst, send_sem=ssem, recv_sem=rsem, device_id=to, device_id_type=MESH
        )
        c.start()
        return c

    def got(ref, rsem, ssem):
        pltpu.make_async_remote_copy(
            src_ref=ref, dst_ref=ref, send_sem=ssem, recv_sem=rsem, device_id=sibling, device_id_type=MESH
        ).wait_recv()

    loads = []
    for i in range(4):
        c = pltpu.make_async_copy(counts.at[pl.ds(i * T, T)], cbuf.at[pl.ds(i * T, T)], csem.at[i])
        c.start()
        loads.append(c)

    barrier = pltpu.get_barrier_semaphore()
    partners = [at_x(d) for d in (1, 2, 3)] + [at_y(d) for d in (1, 2, 3)] + [at_z(d) for d in (1, 2, 3)] + [sibling]
    for to in partners:
        pl.semaphore_signal(barrier, inc=1, device_id=to, device_id_type=MESH)
    pl.semaphore_wait(barrier, len(partners))

    sent = []

    def zblk(d):
        return cg.at[(z + d) % 4, core]

    own_c = pltpu.make_async_copy(cemb, zblk(0), lsem.at[0])
    own_c.start()
    own_rows = []
    for h in range(2):
        c = pltpu.make_async_copy(remb.at[pl.ds(64 * h, 64)], rg.at[y, x, h], lsem.at[1 + h])
        c.start()
        own_rows.append(c)
    sent.append(send(cemb, zblk(0), zs.at[0], zr.at[0], at_z(1)))
    sent.append(send(cemb, zblk(0), zs.at[1], zr.at[1], at_z(3)))
    sent.append(send(cemb, zblk(0), ks.at[0], kr.at[0], sibling))

    def blk(h, first, second):
        if h == 0:
            return rg.at[(y + second) % 4, (x + first) % 4, h]
        return rg.at[(y + first) % 4, (x + second) % 4, h]

    def first_axis(h, d):
        return at_x(d) if h == 0 else at_y(d)

    def second_axis(h, d):
        return at_y(d) if h == 0 else at_x(d)

    for h in range(2):
        own = remb.at[pl.ds(64 * h, 64)]
        sent.append(send(own, blk(h, 0, 0), xs.at[h, 0], xr.at[h, 0], first_axis(h, 1)))
        sent.append(send(own, blk(h, 0, 0), xs.at[h, 1], xr.at[h, 1], first_axis(h, 3)))
    for h in range(2):
        own = remb.at[pl.ds(64 * h, 64)]
        sent.append(send(own, blk(h, 0, 0), ys.at[h, 0, 0], yr.at[h, 0, 0], second_axis(h, 1)))
        sent.append(send(own, blk(h, 0, 0), ys.at[h, 0, 1], yr.at[h, 0, 1], second_axis(h, 3)))

    lo, hi = pl.ds(0, 32), pl.ds(32, 32)
    for h in range(2):
        got(blk(h, 3, 0), xr.at[h, 0], xs.at[h, 0])
        sent.append(send(blk(h, 3, 0).at[lo], blk(h, 3, 0).at[lo], xs.at[h, 2], xr.at[h, 2], first_axis(h, 1)))
        got(blk(h, 1, 0), xr.at[h, 1], xs.at[h, 1])
        sent.append(send(blk(h, 1, 0).at[hi], blk(h, 1, 0).at[hi], xs.at[h, 3], xr.at[h, 3], first_axis(h, 3)))
    for h in range(2):
        for k, f in ((1, 3), (2, 1)):
            sent.append(send(blk(h, f, 0), blk(h, f, 0), ys.at[h, k, 0], yr.at[h, k, 0], second_axis(h, 1)))
            sent.append(send(blk(h, f, 0), blk(h, f, 0), ys.at[h, k, 1], yr.at[h, k, 1], second_axis(h, 3)))
    zlo, zhi = pl.ds(0, 128), pl.ds(128, 128)
    got(zblk(3), zr.at[0], zs.at[0])
    sent.append(send(zblk(3).at[zlo], zblk(3).at[zlo], zs.at[2], zr.at[2], at_z(1)))
    sent.append(send(zblk(3), zblk(3), ks.at[1], kr.at[1], sibling))
    got(zblk(1), zr.at[1], zs.at[1])
    sent.append(send(zblk(1).at[zhi], zblk(1).at[zhi], zs.at[3], zr.at[3], at_z(3)))
    sent.append(send(zblk(1), zblk(1), ks.at[2], kr.at[2], sibling))
    for h in range(2):
        got(blk(h, 2, 0).at[lo], xr.at[h, 2], xs.at[h, 2])
        got(blk(h, 2, 0).at[hi], xr.at[h, 3], xs.at[h, 3])
        sent.append(send(blk(h, 2, 0), blk(h, 2, 0), ys.at[h, 3, 0], yr.at[h, 3, 0], second_axis(h, 1)))
        sent.append(send(blk(h, 2, 0), blk(h, 2, 0), ys.at[h, 3, 1], yr.at[h, 3, 1], second_axis(h, 3)))
    firsts = (0, 3, 1, 2)
    for k in range(4):
        for h in range(2):
            f = firsts[k]
            got(blk(h, f, 3), yr.at[h, k, 0], ys.at[h, k, 0])
            sent.append(send(blk(h, f, 3).at[lo], blk(h, f, 3).at[lo], ys.at[h, k, 2], yr.at[h, k, 2], second_axis(h, 1)))
            got(blk(h, f, 1), yr.at[h, k, 1], ys.at[h, k, 1])
            sent.append(send(blk(h, f, 1).at[hi], blk(h, f, 1).at[hi], ys.at[h, k, 3], yr.at[h, k, 3], second_axis(h, 3)))
    got(zblk(2).at[zlo], zr.at[2], zs.at[2])
    got(zblk(2).at[zhi], zr.at[3], zs.at[3])
    sent.append(send(zblk(2), zblk(2), ks.at[3], kr.at[3], sibling))

    vec[...] = jnp.zeros_like(vec)
    vec[0:1, :] = (rperm[...] - row0).astype(F32)
    vec[1:2, :] = (cperm[...] - col0).astype(F32)
    vec[2:3, :] = rlog[...]

    def turn(i, _):
        o = pl.multiple_of(i * 128, 128)
        vcol[pl.ds(o, 128), :] = jnp.transpose(vec[:, pl.ds(o, 128)])
        return 0

    lax.fori_loop(0, 16, turn, 0)

    own_c.wait()
    for k, d in enumerate((0, 3, 1, 2)):
        got(cg.at[(z + d) % 4, 1 - core], kr.at[k], ks.at[k])

    lane = lax.broadcasted_iota(jnp.int32, (T, SR), 1).astype(F32)

    def pick(i, which, src):
        o = pl.multiple_of(i * T, T)
        hot = jnp.where(vcol[pl.ds(o, T), which : which + 1] == lane, 1.0, 0.0).astype(BF16)
        return dot(hot, src, NN).astype(BF16)

    def pick_c(i, _):
        cvec[pl.ds(pl.multiple_of(i * T, T), T), :] = pick(i, 1, cg[...].reshape(SR, D))
        return 0

    lax.fori_loop(0, 4, pick_c, 0)

    for c in own_rows:
        c.wait()
    for k in range(4):
        for h in range(2):
            f = firsts[k]
            got(blk(h, f, 2).at[lo], yr.at[h, k, 2], ys.at[h, k, 2])
            got(blk(h, f, 2).at[hi], yr.at[h, k, 3], ys.at[h, k, 3])

    def pick_w(i, _):
        o = pl.multiple_of(i * T, T)
        w = pick(i, 0, rg[...].reshape(SR, D))
        wvec[pl.ds(o, T), :] = w
        for h in range(2):
            wt[(core + h) % 2, :, pl.ds(o, T)] = jnp.transpose(w[:, HALF * h : HALF * (h + 1)])
        return 0

    lax.fori_loop(0, 4, pick_w, 0)

    for c in loads:
        c.wait()

    def cells(j, _):
        at = pl.ds(pl.multiple_of(j * BLK, BLK), BLK)
        score = dot(wvec[...], cvec[at, :], NT)
        for i in range(8):
            rows = slice(i * BLK, (i + 1) * BLK)
            count = cbuf[rows, at].astype(F32)
            safe = jnp.maximum(count, 1.0)
            base = vcol[rows, 2:3] + clog[:, at]
            u = score[rows] - (jnp.log(safe) - base)
            pos = (0.1 + 0.25 * (safe * lax.rsqrt(safe))) * u
            zero = 0.5 * jnp.tanh(0.5 * u) + 0.5
            on = mask[i, j].astype(F32)
            delta[rows, at] = (on * jnp.where(count > 0.0, pos, zero)).astype(BF16)
        return 0

    lax.fori_loop(0, 8, cells, 0)

    kcopies = []
    for j in range(4):
        js = pl.ds(j * T, T)
        ht = dot(wt[...].reshape(D, SR), delta[:, js], NN) * h_scale
        hown[j] = ht[:HALF]
        hsend[j] = ht[HALF:]
        kcopies.append(send(hsend.at[j], hrecv.at[j], hks.at[j], hkr.at[j], sibling))
    sent += kcopies

    sub = lax.broadcasted_iota(jnp.int32, (T, SR), 0).astype(F32)

    def spread(k, which):
        at = vec[which : which + 1, :] - lax.convert_element_type(k * T, F32)
        return jnp.where(sub == at, 1.0, 0.0).astype(BF16)

    def row_terms(ch):
        def terms(i, _):
            o = pl.multiple_of(i * T, T)
            gs[pl.ds(o, T), :] = (
                dot(delta[pl.ds(o, T), :], cvec[:, HALF * ch : HALF * (ch + 1)], NN) * g_scale
            ).astype(BF16)
            return 0

        lax.fori_loop(0, 4, terms, 0)

        def order(k, _):
            gord[ch, k] = dot(spread(k, 0), gs[...], NN).astype(BF16).reshape(4, 2, 64, HALF)
            return 0

        lax.fori_loop(0, 4, order, 0)
        for d in (2, 1, 3):
            sent.append(send(gord.at[ch, (y + d) % 4, :, 0], r1.at[ch, 0, d - 1], g1s.at[ch, 0, d - 1], g1r.at[ch, 0, d - 1], at_y(d)))
            sent.append(send(gord.at[ch, :, (x + d) % 4, 1], r1.at[ch, 1, d - 1], g1s.at[ch, 1, d - 1], g1r.at[ch, 1, d - 1], at_x(d)))

    row_terms(0)

    for j in range(4):
        got(hrecv.at[j], hkr.at[j], hks.at[j])
        hb[:, j * T : (j + 1) * T] = (hown[j] + hrecv[j]).astype(BF16)

    def order_c(k, _):
        hord[k] = dot(spread(k, 1), hb[...], NT).astype(BF16).reshape(2, BLK, HALF)
        return 0

    lax.fori_loop(0, 4, order_c, 0)
    for d in (2, 1, 3):
        sent.append(send(hord.at[(z + d) % 4], rz.at[d - 1], hzs.at[d - 1], hzr.at[d - 1], at_z(d)))

    row_terms(1)

    def row_sums(ch):
        for h in range(2):
            for d in range(3):
                got(r1.at[ch, h, d], g1r.at[ch, h, d], g1s.at[ch, h, d])
            mine = gord[ch, y, :, 0] if h == 0 else gord[ch, :, x, 1]
            total = mine.astype(F32)
            for d in range(3):
                total = total + r1[ch, h, d].astype(F32)
            s2[ch, h] = total
            s2b[ch, h] = total.astype(BF16)
            here = x if h == 0 else y
            for d in (2, 1, 3):
                sent.append(send(s2b.at[ch, h, (here + d) % 4], r2.at[ch, h, d - 1], g2s.at[ch, h, d - 1], g2r.at[ch, h, d - 1], second(h, d)))

    def second(h, d):
        return at_x(d) if h == 0 else at_y(d)

    row_sums(0)
    row_sums(1)

    for d in range(3):
        got(rz.at[d], hzr.at[d], hzs.at[d])

    def col_total(k):
        total = hord[z, k].astype(F32)
        for d in range(3):
            total = total + rz[d, k].astype(F32)
        return total

    fsend[...] = col_total(1 - core)
    sent.append(send(fsend, frecv, fsm, frm, sibling))
    cout[:, pl.ds(pl.multiple_of(core * HALF, HALF), HALF)] = col_total(core)

    for ch in range(2):
        for h in range(2):
            for d in range(3):
                got(r2.at[ch, h, d], g2r.at[ch, h, d], g2s.at[ch, h, d])
            here = x if h == 0 else y
            total = s2[ch, h, here]
            for d in range(3):
                total = total + r2[ch, h, d].astype(F32)
            rout[h * 64 : (h + 1) * 64, ch * HALF : (ch + 1) * HALF] = total

    got(frecv, frm, fsm)
    cout[:, pl.ds(pl.multiple_of((1 - core) * HALF, HALF), HALF)] = frecv[...]
    for c in sent:
        c.wait_send()


def shards(counts, block_mask, row_perm, col_perm, row_logm, col_logm, row_emb, col_emb):
    all_cols = counts.shape[1] * lax.axis_size("col")
    all_rows = counts.shape[0] * lax.axis_size("row")
    vm = pl.BlockSpec(memory_space=pltpu.VMEM)
    dma = pltpu.SemaphoreType.DMA
    V = pltpu.VMEM
    rout, cout = pl.pallas_call(
        functools.partial(kernel, float(all_cols) ** -0.5, float(all_rows) ** -0.5),
        out_shape=(
            jax.ShapeDtypeStruct((128, D), F32),
            jax.ShapeDtypeStruct((BLK, D), F32),
        ),
        in_specs=[pl.BlockSpec(memory_space=pl.ANY), pl.BlockSpec(memory_space=pltpu.SMEM)] + [vm] * 6,
        out_specs=(vm, vm),
        scratch_shapes=[
            V((SR, SR), jnp.int32),
            V((4, 4, 2, 64, D), BF16),
            V((4, 2, BLK, D), BF16),
            V((8, SR), F32),
            V((SR, 8), F32),
            V((SR, D), BF16),
            V((2, HALF, SR), BF16),
            V((SR, D), BF16),
            V((SR, SR), BF16),
            V((SR, HALF), BF16),
            V((2, 4, 4, 2, 64, HALF), BF16),
            V((2, 2, 3, 4, 64, HALF), BF16),
            V((2, 2, 4, 64, HALF), F32),
            V((2, 2, 4, 64, HALF), BF16),
            V((2, 2, 3, 64, HALF), BF16),
            V((4, HALF, T), F32),
            V((4, HALF, T), F32),
            V((4, HALF, T), F32),
            V((HALF, SR), BF16),
            V((4, 2, BLK, HALF), BF16),
            V((3, 2, BLK, HALF), BF16),
            V((BLK, HALF), F32),
            V((BLK, HALF), F32),
            dma((4,)),
            dma((2, 4)), dma((2, 4)),
            dma((2, 4, 4)), dma((2, 4, 4)),
            dma((4,)), dma((4,)),
            dma((4,)), dma((4,)),
            dma((3,)),
            dma((2, 2, 3)), dma((2, 2, 3)),
            dma((2, 2, 3)), dma((2, 2, 3)),
            dma((4,)), dma((4,)),
            dma((3,)), dma((3,)),
            dma, dma,
        ],
        compiler_params=pltpu.CompilerParams(
            collective_id=0, has_side_effects=True, vmem_limit_bytes=63 * 1024 * 1024
        ),
        cost_estimate=pl.CostEstimate(flops=26_000_000_000, bytes_accessed=20_000_000, transcendentals=12_000_000),
    )(
        counts, block_mask, row_perm.reshape(1, SR), col_perm.reshape(1, SR),
        row_logm.reshape(1, SR), col_logm.reshape(1, SR), row_emb, col_emb,
    )
    return rout, cout


def solution(mesh):
    in_specs = (
        P("row", "col"),
        P("row", "col"),
        P("row"),
        P("col"),
        P("row"),
        P("col"),
        P(("row", "col"), None),
        P(("col", "row"), None),
    )
    out_specs = (P(("row", "col"), None), P(("col", "row"), None))
    return jax.shard_map(shards, mesh=mesh, in_specs=in_specs, out_specs=out_specs, check_vma=False)
```
